32 devices in a mesh: seq: 16 (over z, y, x), head: 2 (over core).
Axes of the slice: x: 2, y: 2, z: 4, core: 2. Of those that a mesh axis runs over, the one named last changes fastest.
Arguments:
- q_in: bfloat16 [2048, 2048], P('seq', 'head'), may hold values from -6 to 6
- k_in: bfloat16 [2048, 2048], P('seq', 'head'), may hold values from -6 to 6
- v_in: bfloat16 [2048, 2048], P('seq', 'head'), may hold values from -8 to 8
- filters: bfloat16 [3, 128, 128], P(None, 'head'), may hold values from -1 to 1
- lengths: int32 [32], replicated, may hold values from 1 to 128, 2048 in all
- gain: bfloat16 [2048], P('head'), may hold values from 0.099609375 to 1.8984375
Outputs:
- normed: bfloat16 [2048, 2048], P('seq', 'head')
The draws below stay inside these ranges and needn't reach their ends.
Inputs may be any that keep to these rules, and one draw needn't show every extreme that they name: lengths of the 32 documents packed in order along the sequence; they sum to 2048.
All inputs are finite; a program needn't handle non-finite values.
Results may differ from the reference program's by a relative error of at most 0.005.
The reference program's roundings to bfloat16 on the way (of `queries`, `keys`, `values`, `rounded` and `attended`) count: a program that leaves them out, or rounds other values in their place, can miss the bound.
Values may be sent and summed in bfloat16 or wider, within the bound.
No kernel may reach another device: no remote copies, remote signals or barrier semaphores. Data moves between devices by JAX's collectives and lax.ppermute only.
A program may use at most 128 MiB of HBM per device.

```python
import math
import jax
import jax.numpy as jnp
import numpy as np
from jax import lax

HDIM = 128
TAPS = 128
TOK_DEV = 128
HEADS = 16
CHANNELS = 2048
GROUPS = 128
TOKENS = 2048
NDOCS = 32


def drawn_input(key, salt):
    channels = HEADS * HDIM
    base = jnp.clip(jax.random.normal(jax.random.fold_in(key, salt), (TOKENS, channels), jnp.float32), -6.0, 6.0)
    return base.astype(jnp.bfloat16)


def draw_q_in(key, part):
    return drawn_input(key, 1)


def draw_k_in(key, part):
    return drawn_input(key, 2)


def draw_v_in(key, part):
    channels = HEADS * HDIM
    ramp = jnp.arange(channels, dtype=jnp.int32).astype(jnp.float32) / channels
    column_key = jax.random.fold_in(key, 31)
    noise_key = jax.random.fold_in(key, 32)
    column = 3.0 ** (0.5 * ramp) * jax.random.uniform(column_key, (channels,), jnp.float32, 0.8, 1.25)
    noise = jnp.clip(jax.random.normal(noise_key, (TOKENS, channels), jnp.float32), -3.5, 3.5)
    return jnp.clip(noise * column[None, :], -8.0, 8.0).astype(jnp.bfloat16)


def draw_filters(key, part):
    shape = (3, GROUPS, TAPS)
    noise = jax.random.normal(jax.random.fold_in(key, 41), shape, jnp.float32)
    taps = noise / jnp.sqrt(float(TAPS))
    return jnp.clip(taps, -1.0, 1.0).astype(jnp.bfloat16)


def profile(amount, total, reach, slope):
    weights = [(1 << 20) // math.isqrt(grade ** slope) + 1 for grade in range(2, amount + 1)]
    surplus, holding = total - reach - (amount - 1), [1] * (amount - 1)
    while surplus > 0:
        candidates = [i for i in range(amount - 1) if holding[i] < reach]
        mass, budget = sum([weights[i] for i in candidates]), surplus
        for i in candidates:
            more = min(reach - holding[i], max(1, budget * weights[i] // mass), surplus)
            holding[i] = holding[i] + more
            surplus = surplus - more
    return np.array([reach] + holding)


def ragged(rng, number_of, total, most, skew):
    if number_of == 2:
        one = jax.random.randint(rng, (), max(1, total - most), min(most, total - 1) + 1)
        return jnp.stack([one, total - one])
    sizes = jnp.asarray(profile(number_of, total, most, skew), jnp.int32)
    twos = (number_of - 1) // 2
    source_of, sink = sizes[1:1 + 2 * twos:2], sizes[2:2 + 2 * twos:2]
    slack = jnp.minimum(source_of - 1, most - sink)
    passed = jax.random.randint(jax.random.fold_in(rng, 1), (twos,), 0, 1 << 20) % (slack + 1)
    sizes = sizes.at[1:1 + 2 * twos:2].set(source_of - passed).at[2:2 + 2 * twos:2].set(sink + passed)
    return sizes[jax.random.permutation(jax.random.fold_in(rng, 2), number_of)]


def setup_inputs(seed: int = 0) -> dict:
    key_list = jax.random.split(jax.random.key(seed), 7)
    q_in = draw_q_in(jax.random.fold_in(key_list[6], 71), 0)
    k_in = draw_k_in(jax.random.fold_in(key_list[6], 71), 0)
    v_in = draw_v_in(jax.random.fold_in(key_list[6], 71), 0)
    filters = draw_filters(jax.random.fold_in(key_list[6], 71), 0)
    lengths = ragged(key_list[4], NDOCS, TOKENS, TOK_DEV, 2).astype(jnp.int32)
    gain = jnp.clip(1.0 + 0.18 * jax.random.normal(key_list[5], (CHANNELS,), jnp.float32), 0.099609375, 1.8984375).astype(jnp.bfloat16)
    return {"q_in": q_in, "k_in": k_in, "v_in": v_in, "filters": filters, "lengths": lengths, "gain": gain}


def banded(filter_rows, tap_count):
    lag_index = jnp.arange(tap_count, dtype=jnp.int32)[:, None] - jnp.arange(tap_count, dtype=jnp.int32)[None, :]
    within = filter_rows[:, jnp.clip(lag_index, 0, tap_count - 1)]
    beyond = filter_rows[:, jnp.clip(lag_index + tap_count, 0, tap_count - 1)]
    current = jnp.where(lag_index[None] >= 0, within, jnp.zeros_like(within))
    earlier = jnp.where(lag_index[None] < 0, beyond, jnp.zeros_like(beyond))
    return (current, earlier)

def gated_conv(signal, filter_rows):
    tok_count, channels = signal.shape
    groups, tap_count = filter_rows.shape
    widened = signal.astype(jnp.float32)
    blocks = widened.reshape(tok_count // tap_count, tap_count, groups, channels // groups)
    shifted = jnp.concatenate([jnp.zeros_like(blocks[:1]), blocks[:-1]], 0)
    current, earlier = banded(filter_rows.astype(jnp.float32), tap_count)
    convolved = jnp.einsum('gij,bjgc->bigc', current, blocks, precision=lax.Precision.HIGHEST)
    convolved = convolved + jnp.einsum('gij,bjgc->bigc', earlier, shifted, precision=lax.Precision.HIGHEST)
    gated = widened * convolved.reshape(tok_count, channels)
    return lax.optimization_barrier(gated.astype(jnp.bfloat16))

def doc_index(positions, doc_ends):
    return lax.optimization_barrier(jnp.sum((doc_ends[None, :] <= positions[:, None]).astype(jnp.int32), axis=1))

def reference(q_in, k_in, v_in, filters, lengths, gain):
    queries = gated_conv(q_in, filters[0])
    keys = gated_conv(k_in, filters[1])
    values = gated_conv(v_in, filters[2])
    doc_ends = jnp.cumsum(lengths).astype(jnp.int32)
    span = TOK_DEV // 2
    stretch_count = TOKENS // span
    channels = queries.shape[1]
    head_count = channels // HDIM
    padding = jnp.zeros((TOK_DEV, channels), jnp.bfloat16)
    key_pad = jnp.concatenate([padding, keys], 0)
    value_pad = jnp.concatenate([padding, values], 0)
    factor = 1.0 / math.sqrt(HDIM)

    def one_stretch(index):
        start = (index * span).astype(jnp.int32)
        q_rows = lax.dynamic_slice_in_dim(queries, start, span, 0)
        k_rows = lax.dynamic_slice_in_dim(key_pad, start, TOK_DEV + span, 0)
        v_rows = lax.dynamic_slice_in_dim(value_pad, start, TOK_DEV + span, 0)
        q_pos = start + jnp.arange(span, dtype=jnp.int32)
        k_pos = start - TOK_DEV + jnp.arange(TOK_DEV + span, dtype=jnp.int32)
        allowed = doc_index(q_pos, doc_ends)[:, None] == doc_index(k_pos, doc_ends)[None, :]
        allowed = allowed & (k_pos[None, :] <= q_pos[:, None]) & (k_pos[None, :] >= 0)
        q_float = q_rows.astype(jnp.float32).reshape(span, head_count, HDIM)
        k_float = k_rows.astype(jnp.float32).reshape(TOK_DEV + span, head_count, HDIM)
        v_float = v_rows.astype(jnp.float32).reshape(TOK_DEV + span, head_count, HDIM)
        scores = jnp.einsum('qhd,khd->hqk', q_float, k_float, precision=lax.Precision.HIGHEST) * factor
        scores = jnp.where(allowed[None], scores, -1e+30)
        top_score = lax.optimization_barrier(jnp.max(scores, axis=2, keepdims=True))
        weights = jnp.exp(scores - top_score)
        totals = lax.optimization_barrier(jnp.sum(weights, axis=2))
        rounded = lax.optimization_barrier(weights.astype(jnp.bfloat16)).astype(jnp.float32)
        mixed = jnp.einsum('hqk,khd->qhd', rounded, v_float, precision=lax.Precision.HIGHEST)
        mixed = mixed / jnp.transpose(totals)[:, :, None]
        return mixed.reshape(span, channels).astype(jnp.bfloat16)
    attended = lax.map(one_stretch, jnp.arange(stretch_count, dtype=jnp.int32)).reshape(TOKENS, channels)
    widened = lax.optimization_barrier(attended).astype(jnp.float32)
    mean_square = lax.optimization_barrier(jnp.mean(widened * widened, axis=1, keepdims=True))
    normed = widened * lax.rsqrt(mean_square + 1e-06) * gain.astype(jnp.float32)[None, :]
    return normed.astype(jnp.bfloat16)
```

```python
import math

import jax
import jax.numpy as jnp
from jax import lax
from jax.experimental import pallas as pl
from jax.experimental.pallas import tpu as pltpu
from jax.sharding import PartitionSpec as P

HDIM = 128
TEAM = 4
VMEM = pltpu.VMEM
F32 = jnp.float32
BF16 = jnp.bfloat16


def kernel_call(body, outs, args, scratch=(), flops=0):
    spec = pl.BlockSpec(memory_space=VMEM)
    moved = sum(math.prod(a.shape) * a.dtype.itemsize for a in list(args) + list(outs))
    return pl.pallas_call(
        body,
        out_shape=outs,
        in_specs=[spec] * len(args),
        out_specs=[spec] * len(outs),
        scratch_shapes=list(scratch),
        compiler_params=pltpu.CompilerParams(vmem_limit_bytes=48 * 1024 * 1024),
        cost_estimate=pl.CostEstimate(flops=flops, bytes_accessed=moved, transcendentals=0),
    )(*args)


def place():
    return lax.rem(lax.axis_index("seq"), TEAM)


def cut_parts(arrays):
    tokens, channels = arrays[0].shape
    share = channels // TEAM
    count = len(arrays)

    def body(*refs):
        ins, outs = refs[:count], refs[count:]
        me = place()
        for step in range(TEAM):
            first = pl.multiple_of(lax.bitwise_xor(me, step) * share, share)
            for i, ref in enumerate(ins):
                outs[step][i * share : (i + 1) * share, :] = ref[:, pl.ds(first, share)].T

    outs = [jax.ShapeDtypeStruct((count * share, tokens), BF16)] * TEAM
    return kernel_call(body, outs, arrays)


def bands(row):
    taps = row.shape[1]
    turned = pltpu.roll(jnp.broadcast_to(row, (taps, taps)), 0, 1, stride=1, stride_axis=0)
    lag = lax.broadcasted_iota(jnp.int32, (taps, taps), 1) - lax.broadcasted_iota(
        jnp.int32, (taps, taps), 0
    )
    zero = jnp.zeros_like(turned)
    earlier = jnp.where(lag < 0, turned, zero).astype(BF16)
    current = jnp.where(lag >= 0, turned, zero).astype(BF16)
    return jnp.concatenate([earlier, current], 0)


def attend_head(q_cols, k_rows, v_cols, starts, key_shift):
    span, tokens = k_rows.shape[0], q_cols.shape[1]
    scores = jnp.dot(k_rows, q_cols, preferred_element_type=F32) * (1.0 / math.sqrt(HDIM))
    key_pos = lax.broadcasted_iota(jnp.int32, (span, tokens), 0) + key_shift
    query_pos = lax.broadcasted_iota(jnp.int32, (span, tokens), 1)
    allowed = (key_pos >= starts) & (key_pos <= query_pos)
    scores = jnp.where(allowed, scores, -1e30)
    weights = jnp.exp(scores - jnp.max(scores, axis=0, keepdims=True))
    totals = jnp.sum(weights, axis=0, keepdims=True)
    mixed = jnp.dot(v_cols, weights.astype(BF16), preferred_element_type=F32)
    return (mixed / totals).astype(BF16)


def gated(x_now, conv):
    return (x_now.astype(F32) * conv).astype(BF16)


def inner_part(q_parts, kv_parts, filters, starts):
    share, tokens = q_parts[0].shape
    _, groups, taps = filters.shape
    team_groups = groups // TEAM
    width = share // team_groups
    heads = share // HDIM

    def body(*refs):
        q_refs, kv_refs = refs[:TEAM], refs[TEAM : 2 * TEAM]
        filter_ref, starts_ref = refs[2 * TEAM : 2 * TEAM + 2]
        late_ref, raw_ref, q1_ref, k1_ref, v1_ref = refs[2 * TEAM + 2 : 2 * TEAM + 7]
        x_ref, y_ref = refs[2 * TEAM + 7 :]
        me = place()
        for step in range(TEAM):
            block = lax.bitwise_xor(me, step)
            x_ref[block, 0] = q_refs[step][...]
            x_ref[block, 1] = kv_refs[step][:share]
            x_ref[block, 2] = kv_refs[step][share:]
        raw_ref[...] = x_ref[0]
        for part in range(3):
            first = pl.multiple_of(me * team_groups, team_groups)
            rows = filter_ref[part, pl.ds(first, team_groups), :].astype(F32)
            for group in range(team_groups):
                at = slice(group * width, (group + 1) * width)
                band = bands(rows[group : group + 1])
                left = jnp.concatenate(
                    [
                        jnp.concatenate([x_ref[b - 1, part, at], x_ref[b, part, at]], 1)
                        for b in range(1, TEAM)
                    ],
                    0,
                )
                conv = jnp.dot(left, band, preferred_element_type=F32)
                for b in range(1, TEAM):
                    y_ref[part, at, (b - 1) * tokens : b * tokens] = gated(
                        x_ref[b, part, at], conv[(b - 1) * width : b * width]
                    )
        q1_ref[...] = y_ref[0, :, :tokens]
        v1_ref[...] = y_ref[2, :, :tokens]
        for head in range(heads):
            at = slice(head * HDIM, (head + 1) * HDIM)
            keys = [y_ref[1, at, b * tokens : (b + 1) * tokens].T for b in range(TEAM - 1)]
            k1_ref[:, at] = keys[0]
            for b in range(2, TEAM):
                out = attend_head(
                    y_ref[0, at, (b - 1) * tokens : b * tokens],
                    jnp.concatenate([keys[b - 2], keys[b - 1]], 0),
                    y_ref[2, at, (b - 2) * tokens : b * tokens],
                    starts_ref[b : b + 1, :],
                    -tokens,
                )
                late_ref[b - 2, :, at] = out.T

    sds = jax.ShapeDtypeStruct
    outs = [
        sds((TEAM - 2, tokens, share), BF16),
        sds((3, share, tokens), BF16),
        sds((share, tokens), BF16),
        sds((tokens, share), BF16),
        sds((share, tokens), BF16),
    ]
    scratch = [
        VMEM((TEAM, 3, share, tokens), BF16),
        VMEM((3, share, (TEAM - 1) * tokens), BF16),
    ]
    flops = 2 * 3 * share * tokens * 2 * tokens * 4
    return kernel_call(
        body, outs, list(q_parts) + list(kv_parts) + [filters, starts], scratch, flops
    )


def rim_part(rim_q, rim_kv, raw, q1, k1, v1, late, filters, starts):
    share, tokens = rim_q.shape
    _, groups, taps = filters.shape
    team_groups = groups // TEAM
    width = share // team_groups
    heads = share // HDIM

    def body(*refs):
        rq_ref, rkv_ref, raw_ref, q1_ref, k1_ref, v1_ref, late_ref, filter_ref, starts_ref = refs[:9]
        outs = refs[9 : 9 + TEAM]
        y_ref, done_ref = refs[9 + TEAM :]
        me = place()
        for part in range(3):
            first = pl.multiple_of(me * team_groups, team_groups)
            rows = filter_ref[part, pl.ds(first, team_groups), :].astype(F32)
            for group in range(team_groups):
                at = slice(group * width, (group + 1) * width)
                band = bands(rows[group : group + 1])
                now = raw_ref[part, at]
                if part == 0:
                    left = jnp.concatenate([rq_ref[at], now], 1)
                    conv = jnp.dot(left, band, preferred_element_type=F32)
                    y_ref[0, at, tokens:] = gated(now, conv)
                    continue
                base = (part - 1) * share + group * width
                before = rkv_ref[base : base + width]
                further = rkv_ref[2 * share + base : 2 * share + base + width]
                left = jnp.concatenate(
                    [jnp.concatenate([further, before], 1), jnp.concatenate([before, now], 1)], 0
                )
                conv = jnp.dot(left, band, preferred_element_type=F32)
                y_ref[part, at, :tokens] = gated(before, conv[:width])
                y_ref[part, at, tokens:] = gated(now, conv[width:])
        done_ref[2:] = late_ref[...]
        for head in range(heads):
            at = slice(head * HDIM, (head + 1) * HDIM)
            k_far = y_ref[1, at, :tokens].T
            k_now = y_ref[1, at, tokens:].T
            out = attend_head(
                y_ref[0, at, tokens:],
                jnp.concatenate([k_far, k_now], 0),
                y_ref[2, at, :],
                starts_ref[0:1, :],
                -tokens,
            )
            done_ref[0, :, at] = out.T
            out = attend_head(
                q1_ref[at, :],
                jnp.concatenate([k_now, k1_ref[:, at]], 0),
                jnp.concatenate([y_ref[2, at, tokens:], v1_ref[at, :]], 1),
                starts_ref[1:2, :],
                -tokens,
            )
            done_ref[1, :, at] = out.T
        for step in range(TEAM):
            outs[step][...] = done_ref[lax.bitwise_xor(me, step)]

    outs = [jax.ShapeDtypeStruct((tokens, share), BF16)] * TEAM
    scratch = [
        VMEM((3, share, 2 * tokens), BF16),
        VMEM((TEAM, tokens, share), BF16),
    ]
    args = [rim_q, rim_kv, raw, q1, k1, v1, late, filters, starts]
    return kernel_call(body, outs, args, scratch)


def square_sums(parts):
    tokens, share = parts[0].shape

    def body(*refs):
        total = jnp.zeros((tokens, 1), F32)
        for ref in refs[:TEAM]:
            wide = ref[...].astype(F32)
            total = total + jnp.sum(wide * wide, axis=1, keepdims=True)
        refs[TEAM][...] = jnp.broadcast_to(total, (tokens, 128))

    return kernel_call(body, [jax.ShapeDtypeStruct((tokens, 128), F32)], parts)[0]


def scaled(parts, sums, gain, total_channels):
    tokens, share = parts[0].shape
    count = len(sums)

    def body(*refs):
        part_refs, sum_refs = refs[:TEAM], refs[TEAM : TEAM + count]
        gain_ref, out_ref = refs[TEAM + count :]
        me = place()
        total = sum_refs[0][...]
        for ref in sum_refs[1:]:
            total = total + ref[...]
        scale = lax.rsqrt(total / total_channels + 1e-06)
        scale = jnp.concatenate([scale] * (share // 128), 1)
        for step in range(TEAM):
            first = pl.multiple_of(lax.bitwise_xor(me, step) * share, share)
            wide = part_refs[step][...].astype(F32)
            wide = wide * scale * gain_ref[:, pl.ds(first, share)].astype(F32)
            out_ref[:, pl.ds(first, share)] = wide.astype(BF16)

    out = jax.ShapeDtypeStruct((tokens, TEAM * share), BF16)
    args = list(parts) + list(sums) + [gain.reshape(1, TEAM * share)]
    return kernel_call(body, [out], args)[0]


def swapped(value, step):
    count = lax.axis_size("seq")
    return lax.ppermute(value, "seq", [(i, i ^ step) for i in range(count)])


def onward(value):
    count = lax.axis_size("seq")
    return lax.ppermute(value, "seq", [(i, i + TEAM) for i in range(count - TEAM)])


def chosen(parts, block):
    return lax.select_n(lax.bitwise_xor(place(), block), *parts)


def document_starts(lengths, tokens):
    ends = jnp.cumsum(lengths)
    base = (lax.axis_index("seq") // TEAM) * (TEAM * tokens)
    pos = base + jnp.arange(TEAM * tokens, dtype=jnp.int32)
    begun = jnp.where(ends[:, None] <= pos[None, :], ends[:, None], 0)
    first = jnp.max(begun, axis=0).reshape(TEAM, tokens)
    block_base = base + tokens * jnp.arange(TEAM, dtype=jnp.int32)
    return first - block_base[:, None]


def per_device(q_in, k_in, v_in, filters, lengths, gain):
    tokens, channels = q_in.shape
    steps = (0, 3, 1, 2)
    kv_cut = cut_parts([k_in, v_in])
    q_cut = cut_parts([q_in])
    kv_parts = list(kv_cut)
    for step in steps[1:]:
        kv_parts[step] = swapped(kv_cut[step], step)
    q_parts = list(q_cut)
    for step in steps[1:]:
        q_parts[step] = swapped(q_cut[step], step)
    starts = document_starts(lengths, tokens)
    rim_kv = onward(jnp.concatenate([chosen(kv_parts, TEAM - 1), chosen(kv_parts, TEAM - 2)], 0))
    rim_q = onward(chosen(q_parts, TEAM - 1))
    late, raw, q1, k1, v1 = inner_part(q_parts, kv_parts, filters, starts)
    made = list(rim_part(rim_q, rim_kv, raw, q1, k1, v1, late, filters, starts))
    mine = list(made)
    for step in steps[1:]:
        mine[step] = swapped(made[step], step)
    own = square_sums(mine)
    head_count = lax.axis_size("head")
    if head_count == 2:
        sums = [own, lax.ppermute(own, "head", [(0, 1), (1, 0)])]
    else:
        sums = [lax.psum(own, "head")]
    return scaled(mine, sums, gain, channels * head_count)


def solution(mesh):
    placed = (
        P("seq", "head"),
        P("seq", "head"),
        P("seq", "head"),
        P(None, "head", None),
        P(),
        P("head"),
    )
    return jax.shard_map(
        per_device, mesh=mesh, in_specs=placed, out_specs=P("seq", "head"), check_vma=False
    )
```

```python
import math

import jax
import jax.numpy as jnp
from jax import lax
from jax.experimental import pallas as pl
from jax.experimental.pallas import tpu as pltpu
from jax.sharding import PartitionSpec as P

HDIM = 128
TEAM = 2
VMEM = pltpu.VMEM
F32 = jnp.float32
BF16 = jnp.bfloat16


def kernel_call(body, outs, args, scratch=(), flops=0, spaces=None, out_spaces=None):
    spaces = spaces or [VMEM] * len(args)
    out_spaces = out_spaces or [VMEM] * len(outs)
    moved = sum(math.prod(a.shape) * a.dtype.itemsize for a in list(args) + list(outs))
    return pl.pallas_call(
        body,
        out_shape=outs,
        in_specs=[pl.BlockSpec(memory_space=space) for space in spaces],
        out_specs=[pl.BlockSpec(memory_space=space) for space in out_spaces],
        scratch_shapes=list(scratch),
        compiler_params=pltpu.CompilerParams(vmem_limit_bytes=40 * 1024 * 1024),
        cost_estimate=pl.CostEstimate(flops=flops, bytes_accessed=moved, transcendentals=0),
    )(*args)


def place():
    return lax.rem(lax.axis_index("seq"), TEAM)


def cut_halves(arrays, stay=True):
    tokens, channels = arrays[0].shape
    share = channels // TEAM
    count = len(arrays)

    def body(*refs):
        ins, outs = refs[:count], refs[count : count + TEAM]
        held, sems = refs[count + TEAM :]
        me = place()
        copies = []
        for step in (1, 0):
            first = pl.multiple_of(lax.bitwise_xor(me, step) * share, share)
            for i, ref in enumerate(ins):
                copy = pltpu.make_async_copy(
                    ref.at[:, pl.ds(first, share)], held.at[i, step], sems.at[i, step]
                )
                copy.start()
                copies.append((copy, i, step))
        for copy, i, step in copies:
            copy.wait()
            outs[step][i * share : (i + 1) * share, :] = held[i, step].T

    outs = [jax.ShapeDtypeStruct((count * share, tokens), BF16)] * TEAM
    scratch = [
        VMEM((count, TEAM, tokens, share), BF16),
        pltpu.SemaphoreType.DMA((count, TEAM)),
    ]
    if stay:
        arrays = [pltpu.with_memory_space_constraint(a, pltpu.HBM) for a in arrays]
    return kernel_call(body, outs, arrays, scratch, spaces=[pl.ANY] * count)


def bands(row):
    taps = row.shape[1]
    turned = pltpu.roll(jnp.broadcast_to(row, (taps, taps)), 0, 1, stride=1, stride_axis=0)
    lag = lax.broadcasted_iota(jnp.int32, (taps, taps), 1) - lax.broadcasted_iota(
        jnp.int32, (taps, taps), 0
    )
    zero = jnp.zeros_like(turned)
    earlier = jnp.where(lag < 0, turned, zero).astype(BF16)
    current = jnp.where(lag >= 0, turned, zero).astype(BF16)
    return jnp.concatenate([earlier, current], 0)


def filter_rows(filter_ref, part, me):
    team_groups = filter_ref.shape[1] // TEAM
    first = pl.multiple_of(me * team_groups, team_groups)
    return filter_ref[part, pl.ds(first, team_groups), :].astype(F32)


def attend_head(q_cols, k_rows, v_cols, starts):
    span, tokens = k_rows.shape[0], q_cols.shape[1]
    scores = jnp.dot(k_rows, q_cols, preferred_element_type=F32) * (1.0 / math.sqrt(HDIM))
    key_pos = lax.broadcasted_iota(jnp.int32, (span, tokens), 0) - tokens
    query_pos = lax.broadcasted_iota(jnp.int32, (span, tokens), 1)
    allowed = (key_pos >= starts) & (key_pos <= query_pos)
    scores = jnp.where(allowed, scores, -1e30)
    weights = jnp.exp(scores - jnp.max(scores, axis=0, keepdims=True))
    totals = jnp.sum(weights, axis=0, keepdims=True)
    mixed = jnp.dot(v_cols, weights.astype(BF16), preferred_element_type=F32)
    return (mixed / totals).astype(BF16)


def gated(x_now, conv):
    return (x_now.astype(F32) * conv).astype(BF16)


def second_conv(q_own, q_got, kv_own, kv_got, filters):
    share, tokens = q_own.shape
    team_groups = filters.shape[1] // TEAM
    width = share // team_groups

    def body(q_own_ref, q_got_ref, kv_own_ref, kv_got_ref, filter_ref, raw_ref, last_ref, q1_ref, k1_ref, v1_ref, x_ref, y_ref):
        me = place()
        other = 1 - me
        x_ref[me, 0] = q_own_ref[...]
        x_ref[me, 1] = kv_own_ref[:share]
        x_ref[me, 2] = kv_own_ref[share:]
        x_ref[other, 0] = q_got_ref[...]
        x_ref[other, 1] = kv_got_ref[:share]
        x_ref[other, 2] = kv_got_ref[share:]
        raw_ref[...] = x_ref[0]
        last_ref[...] = x_ref[1, 0]
        for part in range(3):
            rows = filter_rows(filter_ref, part, me)
            for group in range(team_groups):
                at = slice(group * width, (group + 1) * width)
                now = x_ref[1, part, at]
                left = jnp.concatenate([x_ref[0, part, at], now], 1)
                conv = jnp.dot(left, bands(rows[group : group + 1]), preferred_element_type=F32)
                y_ref[part, at] = gated(now, conv)
        q1_ref[...] = y_ref[0]
        v1_ref[...] = y_ref[2]
        for first in range(0, share, HDIM):
            k1_ref[:, first : first + HDIM] = y_ref[1, first : first + HDIM].T

    sds = jax.ShapeDtypeStruct
    outs = [
        sds((3, share, tokens), BF16),
        sds((share, tokens), BF16),
        sds((share, tokens), BF16),
        sds((tokens, share), BF16),
        sds((share, tokens), BF16),
    ]
    scratch = [VMEM((TEAM, 3, share, tokens), BF16), VMEM((3, share, tokens), BF16)]
    flops = 2 * 3 * share * tokens * 2 * tokens * 8
    return kernel_call(body, outs, [q_own, q_got, kv_own, kv_got, filters], scratch, flops)


def rim_keys(rim_own, rim_got, raw, q1, k1, v1, filters, starts):
    share, tokens = q1.shape
    team_groups = filters.shape[1] // TEAM
    width = share // team_groups

    def body(own_ref, got_ref, raw_ref, q1_ref, k1_ref, v1_ref, filter_ref, starts_ref, k_ref, v_ref, out_ref, rim_ref, y_ref):
        me = place()
        rim_ref[me] = own_ref[...]
        rim_ref[1 - me] = got_ref[...]
        for part in (1, 2):
            rows = filter_rows(filter_ref, part, me)
            for group in range(team_groups):
                at = slice(group * width, (group + 1) * width)
                base = (part - 1) * share + group * width
                further = rim_ref[0, base : base + width]
                before = rim_ref[1, base : base + width]
                now = raw_ref[part, at]
                left = jnp.concatenate(
                    [jnp.concatenate([further, before], 1), jnp.concatenate([before, now], 1)], 0
                )
                conv = jnp.dot(left, bands(rows[group : group + 1]), preferred_element_type=F32)
                far = gated(before, conv[:width])
                near = gated(now, conv[width:])
                if part == 1:
                    y_ref[at, :tokens] = far
                    y_ref[at, tokens:] = near
                else:
                    v_ref[at, :tokens] = far
                    v_ref[at, tokens:] = near
        for first in range(0, share, HDIM):
            at = slice(first, first + HDIM)
            k_ref[:tokens, at] = y_ref[at, :tokens].T
            near = y_ref[at, tokens:].T
            k_ref[tokens:, at] = near
            out = attend_head(
                q1_ref[at, :],
                jnp.concatenate([near, k1_ref[:, at]], 0),
                jnp.concatenate([v_ref[at, tokens:], v1_ref[at, :]], 1),
                starts_ref[1:2, :],
            )
            out_ref[:, at] = out.T

    sds = jax.ShapeDtypeStruct
    outs = [
        sds((2 * tokens, share), BF16),
        sds((share, 2 * tokens), BF16),
        sds((tokens, share), BF16),
    ]
    scratch = [VMEM((TEAM, 2 * share, tokens), BF16), VMEM((share, 2 * tokens), BF16)]
    args = [rim_own, rim_got, raw, q1, k1, v1, filters, starts]
    return kernel_call(body, outs, args, scratch, 2 * 2 * share * tokens * 2 * tokens * 8)


def first_attention(rim_q, raw, keys, values, second, filters, starts):
    share, tokens = rim_q.shape
    team_groups = filters.shape[1] // TEAM
    width = share // team_groups

    def body(rim_ref, raw_ref, k_ref, v_ref, second_ref, filter_ref, starts_ref, keep_ref, send_ref, y_ref, out_ref):
        me = place()
        rows = filter_rows(filter_ref, 0, me)
        for group in range(team_groups):
            at = slice(group * width, (group + 1) * width)
            now = raw_ref[0, at]
            left = jnp.concatenate([rim_ref[at], now], 1)
            conv = jnp.dot(left, bands(rows[group : group + 1]), preferred_element_type=F32)
            y_ref[at] = gated(now, conv)
        for first in range(0, share, HDIM):
            at = slice(first, first + HDIM)
            out = attend_head(y_ref[at], k_ref[:, at], v_ref[at, :], starts_ref[0:1, :])
            out_ref[0, :, at] = out.T
        out_ref[1] = second_ref[...]
        keep_ref[...] = out_ref[me]
        send_ref[...] = out_ref[1 - me]

    outs = [jax.ShapeDtypeStruct((tokens, share), BF16)] * 2
    scratch = [VMEM((share, tokens), BF16), VMEM((TEAM, tokens, share), BF16)]
    args = [rim_q, raw, keys, values, second, filters, starts]
    return kernel_call(body, outs, args, scratch, 2 * share * tokens * 2 * tokens * 8)


def square_sums(parts):
    tokens = parts[0].shape[0]

    def body(*refs):
        total = jnp.zeros((tokens, 1), F32)
        for ref in refs[:-1]:
            wide = ref[...].astype(F32)
            total = total + jnp.sum(wide * wide, axis=1, keepdims=True)
        refs[-1][...] = jnp.broadcast_to(total, (tokens, 128))

    return kernel_call(body, [jax.ShapeDtypeStruct((tokens, 128), F32)], parts)[0]


def scaled(parts, sums, gain, total_channels):
    tokens, share = parts[0].shape
    count = len(sums)

    def body(*refs):
        part_refs, sum_refs = refs[:TEAM], refs[TEAM : TEAM + count]
        gain_ref, out_ref, held, sems = refs[TEAM + count :]
        me = place()
        total = sum_refs[0][...]
        for ref in sum_refs[1:]:
            total = total + ref[...]
        scale = lax.rsqrt(total / total_channels + 1e-06)
        piece = share // 2
        scale = jnp.concatenate([scale] * (piece // 128), 1)
        copies = []
        for step in range(TEAM):
            for cut in range(2):
                at = slice(cut * piece, (cut + 1) * piece)
                first = pl.multiple_of(lax.bitwise_xor(me, step) * share + cut * piece, piece)
                wide = part_refs[step][:, at].astype(F32)
                wide = wide * scale * gain_ref[:, pl.ds(first, piece)].astype(F32)
                held[step, cut] = wide.astype(BF16)
                copy = pltpu.make_async_copy(
                    held.at[step, cut], out_ref.at[:, pl.ds(first, piece)], sems.at[step, cut]
                )
                copy.start()
                copies.append(copy)
        for copy in copies:
            copy.wait()

    out = jax.ShapeDtypeStruct((tokens, TEAM * share), BF16)
    args = list(parts) + list(sums) + [gain.reshape(1, TEAM * share)]
    scratch = [
        VMEM((TEAM, 2, tokens, share // 2), BF16),
        pltpu.SemaphoreType.DMA((TEAM, 2)),
    ]
    return kernel_call(body, [out], args, scratch, out_spaces=[pltpu.HBM])[0]


def swapped(value):
    count = lax.axis_size("seq")
    return lax.ppermute(value, "seq", [(i, i ^ 1) for i in range(count)])


def onward(value):
    count = lax.axis_size("seq")
    return lax.ppermute(value, "seq", [(i, i + TEAM) for i in range(count - TEAM)])


def document_starts(lengths, tokens):
    ends = jnp.cumsum(lengths)
    base = (lax.axis_index("seq") // TEAM) * (TEAM * tokens)
    pos = base + jnp.arange(TEAM * tokens, dtype=jnp.int32)
    begun = jnp.where(ends[:, None] <= pos[None, :], ends[:, None], 0)
    first = jnp.max(begun, axis=0).reshape(TEAM, tokens)
    block_base = base + tokens * jnp.arange(TEAM, dtype=jnp.int32)
    return first - block_base[:, None]


def per_device(q_in, k_in, v_in, filters, lengths, gain):
    tokens, channels = q_in.shape
    kv_own, kv_other = cut_halves([k_in, v_in])
    half = kv_other.shape[0] // 2
    k_got = swapped(kv_other[:half])
    v_got = swapped(kv_other[half:])
    q_own, q_other = cut_halves([q_in], stay=False)
    q_other, k_got = lax.optimization_barrier((q_other, k_got))
    q_got = swapped(q_other)
    rim_own = onward(kv_own)
    kv_got = jnp.concatenate([k_got, v_got], 0)
    rim_got = onward(kv_got)
    starts = document_starts(lengths, tokens)
    raw, last_q, q1, k1, v1 = second_conv(q_own, q_got, kv_own, kv_got, filters)
    rim_q = onward(last_q)
    keys, values, second = rim_keys(rim_own, rim_got, raw, q1, k1, v1, filters, starts)
    keep, send = first_attention(rim_q, raw, keys, values, second, filters, starts)
    mine = [keep, swapped(send)]
    own = square_sums(mine)
    head_count = lax.axis_size("head")
    if head_count == 2:
        sums = [own, lax.ppermute(own, "head", [(0, 1), (1, 0)])]
    else:
        sums = [lax.psum(own, "head")]
    return scaled(mine, sums, gain, channels * head_count)


def solution(mesh):
    placed = (
        P("seq", "head"),
        P("seq", "head"),
        P("seq", "head"),
        P(None, "head", None),
        P(),
        P("head"),
    )
    return jax.shard_map(
        per_device, mesh=mesh, in_specs=placed, out_specs=P("seq", "head"), check_vma=False
    )
```

```python
import math

import jax
import jax.numpy as jnp
from jax import lax
from jax.experimental import pallas as pl
from jax.experimental.pallas import tpu as pltpu
from jax.sharding import PartitionSpec as P

HDIM = 128
TEAM = 2
VMEM = pltpu.VMEM
F32 = jnp.float32
BF16 = jnp.bfloat16


def kernel_call(body, outs, args, scratch=(), flops=0, spaces=None, out_spaces=None):
    spaces = spaces or [VMEM] * len(args)
    out_spaces = out_spaces or [VMEM] * len(outs)
    moved = sum(math.prod(a.shape) * a.dtype.itemsize for a in list(args) + list(outs))
    return pl.pallas_call(
        body,
        out_shape=outs,
        in_specs=[pl.BlockSpec(memory_space=space) for space in spaces],
        out_specs=[pl.BlockSpec(memory_space=space) for space in out_spaces],
        scratch_shapes=list(scratch),
        compiler_params=pltpu.CompilerParams(vmem_limit_bytes=40 * 1024 * 1024),
        cost_estimate=pl.CostEstimate(flops=flops, bytes_accessed=moved, transcendentals=0),
    )(*args)


def place():
    return lax.rem(lax.axis_index("seq"), TEAM)


def cut_halves(arrays, lengths=None):
    tokens, channels = arrays[0].shape
    share = channels // TEAM
    count = len(arrays)
    first_cut = lengths is not None

    def body(*refs):
        ins, refs = refs[:count], refs[count:]
        me = place()
        if first_cut:
            lengths_ref, *outs, starts_ref, held, sems, row_ref, row_sem = refs
            row_copy = pltpu.make_async_copy(lengths_ref, row_ref, row_sem)
            row_copy.start()
        else:
            *outs, held, sems = refs
        copies = []
        for step in (1, 0):
            first = pl.multiple_of(lax.bitwise_xor(me, step) * share, share)
            for i, ref in enumerate(ins):
                copy = pltpu.make_async_copy(
                    ref.at[:, pl.ds(first, share)], held.at[i, step], sems.at[i, step]
                )
                copy.start()
                copies.append((copy, i, step))
        if first_cut:
            row_copy.wait()
            base = (lax.axis_index("seq") - me) * tokens
            starts_ref[...] = document_starts(row_ref[...], base, tokens)
        for copy, i, step in copies:
            copy.wait()
            outs[step][i * share : (i + 1) * share, :] = held[i, step].T

    outs = [jax.ShapeDtypeStruct((count * share, tokens), BF16)] * TEAM
    scratch = [
        VMEM((count, TEAM, tokens, share), BF16),
        pltpu.SemaphoreType.DMA((count, TEAM)),
    ]
    args = list(arrays)
    if first_cut:
        row = lengths.reshape(1, lengths.shape[0])
        args = [pltpu.with_memory_space_constraint(a, pltpu.HBM) for a in args + [row]]
        outs.append(jax.ShapeDtypeStruct((TEAM, tokens), jnp.int32))
        scratch += [VMEM(row.shape, jnp.int32), pltpu.SemaphoreType.DMA]
    return kernel_call(body, outs, args, scratch, spaces=[pl.ANY] * len(args))


def bands(row):
    taps = row.shape[1]
    turned = pltpu.roll(jnp.broadcast_to(row, (taps, taps)), 0, 1, stride=1, stride_axis=0)
    lag = lax.broadcasted_iota(jnp.int32, (taps, taps), 1) - lax.broadcasted_iota(
        jnp.int32, (taps, taps), 0
    )
    zero = jnp.zeros_like(turned)
    earlier = jnp.where(lag < 0, turned, zero).astype(BF16)
    current = jnp.where(lag >= 0, turned, zero).astype(BF16)
    return jnp.concatenate([earlier, current], 0)


def filter_rows(filter_ref, part, me):
    team_groups = filter_ref.shape[1] // TEAM
    first = pl.multiple_of(me * team_groups, team_groups)
    return filter_ref[part, pl.ds(first, team_groups), :].astype(F32)


def attend_head(q_cols, k_rows, v_cols, starts):
    span, tokens = k_rows.shape[0], q_cols.shape[1]
    scores = jnp.dot(k_rows, q_cols, preferred_element_type=F32) * (1.0 / math.sqrt(HDIM))
    key_pos = lax.broadcasted_iota(jnp.int32, (span, tokens), 0) - tokens
    query_pos = lax.broadcasted_iota(jnp.int32, (span, tokens), 1)
    allowed = (key_pos >= starts) & (key_pos <= query_pos)
    scores = jnp.where(allowed, scores, -1e30)
    weights = jnp.exp(scores - jnp.max(scores, axis=0, keepdims=True))
    totals = jnp.sum(weights, axis=0, keepdims=True)
    mixed = jnp.dot(v_cols, weights.astype(BF16), preferred_element_type=F32)
    return (mixed / totals).astype(BF16)


def document_starts(lengths, base, tokens):
    docs = lengths.shape[1]
    until = lax.broadcasted_iota(jnp.int32, (docs, docs), 1) <= lax.broadcasted_iota(
        jnp.int32, (docs, docs), 0
    )
    spread = jnp.broadcast_to(lengths.astype(F32), (docs, docs))
    ends = jnp.sum(jnp.where(until, spread, 0.0), axis=1, keepdims=True)
    rows = []
    for block in range(TEAM):
        first = base + block * tokens
        pos = (lax.broadcasted_iota(jnp.int32, (docs, tokens), 1) + first).astype(F32)
        begun = jnp.max(jnp.where(ends <= pos, ends, 0.0), axis=0, keepdims=True)
        rows.append(begun.astype(jnp.int32) - first)
    return jnp.concatenate(rows, 0)


def gated(x_now, conv):
    return (x_now.astype(F32) * conv).astype(BF16)


def second_queries(q_own, q_got, after):
    def body(own_ref, got_ref, after_ref, out_ref):
        me = place()

        @pl.when(me == 0)
        def _():
            out_ref[...] = got_ref[...]

        @pl.when(me != 0)
        def _():
            out_ref[...] = own_ref[...]

    outs = [jax.ShapeDtypeStruct(q_own.shape, BF16)]
    flops = 2 * 3 * q_own.size * 256 * 8
    return kernel_call(body, outs, [q_own, q_got, after], (), flops, [VMEM, VMEM, pl.ANY])[0]


def second_conv(q_own, q_got, kv_own, kv_got, filters):
    share, tokens = q_own.shape
    team_groups = filters.shape[1] // TEAM
    width = share // team_groups

    def body(q_own_ref, q_got_ref, kv_own_ref, kv_got_ref, filter_ref, raw_ref, q1_ref, k1_ref, v1_ref, x_ref, y_ref):
        me = place()
        other = 1 - me
        x_ref[me, 0] = q_own_ref[...]
        x_ref[me, 1] = kv_own_ref[:share]
        x_ref[me, 2] = kv_own_ref[share:]
        x_ref[other, 0] = q_got_ref[...]
        x_ref[other, 1] = kv_got_ref[:share]
        x_ref[other, 2] = kv_got_ref[share:]
        raw_ref[...] = x_ref[0]
        for part in range(3):
            rows = filter_rows(filter_ref, part, me)
            for group in range(team_groups):
                at = slice(group * width, (group + 1) * width)
                now = x_ref[1, part, at]
                left = jnp.concatenate([x_ref[0, part, at], now], 1)
                conv = jnp.dot(left, bands(rows[group : group + 1]), preferred_element_type=F32)
                y_ref[part, at] = gated(now, conv)
        q1_ref[...] = y_ref[0]
        v1_ref[...] = y_ref[2]
        for first in range(0, share, HDIM):
            k1_ref[:, first : first + HDIM] = y_ref[1, first : first + HDIM].T

    sds = jax.ShapeDtypeStruct
    outs = [
        sds((3, share, tokens), BF16),
        sds((share, tokens), BF16),
        sds((tokens, share), BF16),
        sds((share, tokens), BF16),
    ]
    scratch = [VMEM((TEAM, 3, share, tokens), BF16), VMEM((3, share, tokens), BF16)]
    flops = 2 * 3 * share * tokens * 2 * tokens * 8
    return kernel_call(body, outs, [q_own, q_got, kv_own, kv_got, filters], scratch, flops)


def square_row(head_out):
    wide = head_out.astype(F32)
    return jnp.sum(wide * wide, axis=0, keepdims=True)


def rim_keys(rim_own, rim_got, raw, q1, k1, v1, filters, starts):
    share, tokens = q1.shape
    team_groups = filters.shape[1] // TEAM
    width = share // team_groups

    def body(own_ref, got_ref, raw_ref, q1_ref, k1_ref, v1_ref, filter_ref, starts_ref, k_ref, v_ref, out_ref, sum_ref, rim_ref, y_ref):
        me = place()
        rim_ref[me] = own_ref[...]
        rim_ref[1 - me] = got_ref[...]
        for part in (1, 2):
            rows = filter_rows(filter_ref, part, me)
            for group in range(team_groups):
                at = slice(group * width, (group + 1) * width)
                base = (part - 1) * share + group * width
                further = rim_ref[0, base : base + width]
                before = rim_ref[1, base : base + width]
                now = raw_ref[part, at]
                left = jnp.concatenate(
                    [jnp.concatenate([further, before], 1), jnp.concatenate([before, now], 1)], 0
                )
                conv = jnp.dot(left, bands(rows[group : group + 1]), preferred_element_type=F32)
                far = gated(before, conv[:width])
                near = gated(now, conv[width:])
                if part == 1:
                    y_ref[at, :tokens] = far
                    y_ref[at, tokens:] = near
                else:
                    v_ref[at, :tokens] = far
                    v_ref[at, tokens:] = near
        total = jnp.zeros((1, tokens), F32)
        for first in range(0, share, HDIM):
            at = slice(first, first + HDIM)
            k_ref[:tokens, at] = y_ref[at, :tokens].T
            near = y_ref[at, tokens:].T
            k_ref[tokens:, at] = near
            out = attend_head(
                q1_ref[at, :],
                jnp.concatenate([near, k1_ref[:, at]], 0),
                jnp.concatenate([v_ref[at, tokens:], v1_ref[at, :]], 1),
                starts_ref[1:2, :],
            )
            out_ref[:, at] = out.T
            total = total + square_row(out)
        sum_ref[...] = jnp.broadcast_to(total, (8, tokens))

    sds = jax.ShapeDtypeStruct
    outs = [
        sds((2 * tokens, share), BF16),
        sds((share, 2 * tokens), BF16),
        sds((tokens, share), BF16),
        sds((8, tokens), F32),
    ]
    scratch = [VMEM((TEAM, 2 * share, tokens), BF16), VMEM((share, 2 * tokens), BF16)]
    args = [rim_own, rim_got, raw, q1, k1, v1, filters, starts]
    return kernel_call(body, outs, args, scratch, 2 * 2 * share * tokens * 2 * tokens * 8)


def first_attention(rim_q, raw, keys, values, second, second_sum, filters, starts):
    share, tokens = rim_q.shape
    team_groups = filters.shape[1] // TEAM
    width = share // team_groups

    def body(rim_ref, raw_ref, k_ref, v_ref, second_ref, second_sum_ref, filter_ref, starts_ref, keep_ref, send_ref, sum_ref, y_ref, out_ref):
        me = place()
        rows = filter_rows(filter_ref, 0, me)
        for group in range(team_groups):
            at = slice(group * width, (group + 1) * width)
            now = raw_ref[0, at]
            left = jnp.concatenate([rim_ref[at], now], 1)
            conv = jnp.dot(left, bands(rows[group : group + 1]), preferred_element_type=F32)
            y_ref[at] = gated(now, conv)
        total = jnp.zeros((1, tokens), F32)
        for first in range(0, share, HDIM):
            at = slice(first, first + HDIM)
            out = attend_head(y_ref[at], k_ref[:, at], v_ref[at, :], starts_ref[0:1, :])
            out_ref[0, :, at] = out.T
            total = total + square_row(out)
        out_ref[1] = second_ref[...]
        row = lax.broadcasted_iota(jnp.int32, (8, tokens), 0)
        sum_ref[...] = jnp.where(row == 0, jnp.broadcast_to(total, (8, tokens)), second_sum_ref[...])
        keep_ref[...] = out_ref[me]
        send_ref[...] = out_ref[1 - me]

    outs = [jax.ShapeDtypeStruct((tokens, share), BF16)] * 2
    outs += [jax.ShapeDtypeStruct((8, tokens), F32)]
    scratch = [VMEM((share, tokens), BF16), VMEM((TEAM, tokens, share), BF16)]
    args = [rim_q, raw, keys, values, second, second_sum, filters, starts]
    return kernel_call(body, outs, args, scratch, 2 * share * tokens * 2 * tokens * 8)


def scaled(parts, sums, gain, total_channels, count_got):
    tokens, share = parts[0].shape
    count = len(sums)

    def body(*refs):
        part_refs, sum_refs = refs[:TEAM], refs[TEAM : TEAM + count]
        gain_ref, out_ref, held, sems = refs[TEAM + count :]
        me = place()
        total = jnp.zeros((1, tokens), F32)
        for ref in sum_refs:
            total = total + ref[pl.ds(me, 1), :]
        total = jnp.broadcast_to(total, (128, tokens)).T
        if count_got:
            wide = part_refs[1][...].astype(F32)
            total = total + jnp.sum(wide * wide, axis=1, keepdims=True)
        scale = lax.rsqrt(total / total_channels + 1e-06)
        piece = share // 2
        scale = jnp.concatenate([scale] * (piece // 128), 1)
        copies = []
        for step in range(TEAM):
            for cut in range(2):
                at = slice(cut * piece, (cut + 1) * piece)
                first = pl.multiple_of(lax.bitwise_xor(me, step) * share + cut * piece, piece)
                wide = part_refs[step][:, at].astype(F32)
                wide = wide * scale * gain_ref[:, pl.ds(first, piece)].astype(F32)
                held[step, cut] = wide.astype(BF16)
                copy = pltpu.make_async_copy(
                    held.at[step, cut], out_ref.at[:, pl.ds(first, piece)], sems.at[step, cut]
                )
                copy.start()
                copies.append(copy)
        for copy in copies:
            copy.wait()

    out = jax.ShapeDtypeStruct((tokens, TEAM * share), BF16)
    args = list(parts) + list(sums) + [gain.reshape(1, TEAM * share)]
    scratch = [
        VMEM((TEAM, 2, tokens, share // 2), BF16),
        pltpu.SemaphoreType.DMA((TEAM, 2)),
    ]
    return kernel_call(body, [out], args, scratch, out_spaces=[pltpu.HBM])[0]


def swapped(value):
    count = lax.axis_size("seq")
    return lax.ppermute(value, "seq", [(i, i ^ 1) for i in range(count)])


def onward(value):
    count = lax.axis_size("seq")
    return lax.ppermute(value, "seq", [(i, i + TEAM) for i in range(count - TEAM)])


def per_device(q_in, k_in, v_in, filters, lengths, gain):
    tokens, channels = q_in.shape
    kv_own, kv_other, starts = cut_halves([k_in, v_in], lengths)
    half = kv_other.shape[0] // 2
    k_got = swapped(kv_other[:half])
    v_got = swapped(kv_other[half:])
    q_own, q_other = cut_halves([q_in])
    q_other, k_got = lax.optimization_barrier((q_other, k_got))
    q_got = swapped(q_other)
    rim_own = onward(kv_own)
    kv_got = jnp.concatenate([k_got, v_got], 0)
    rim_got = onward(kv_got)
    rim_q = onward(second_queries(q_own, q_got, kv_got))
    raw, q1, k1, v1 = second_conv(q_own, q_got, kv_own, kv_got, filters)
    keys, values, second, second_sum = rim_keys(rim_own, rim_got, raw, q1, k1, v1, filters, starts)
    keep, send, own = first_attention(
        rim_q, raw, keys, values, second, second_sum, filters, starts
    )
    mine = [keep, swapped(send)]
    head_count = lax.axis_size("head")
    if head_count == 2:
        cross = [(i, i ^ 3) for i in range(2 * lax.axis_size("seq"))]
        sums = [
            own,
            lax.ppermute(own, "head", [(0, 1), (1, 0)]),
            lax.ppermute(own, ("seq", "head"), cross),
        ]
        return scaled(mine, sums, gain, channels * head_count, True)
    own = lax.psum(own, "head")
    return scaled(mine, [own, swapped(own)], gain, channels * head_count, False)


def solution(mesh):
    placed = (
        P("seq", "head"),
        P("seq", "head"),
        P("seq", "head"),
        P(None, "head", None),
        P(),
        P("head"),
    )
    return jax.shard_map(
        per_device, mesh=mesh, in_specs=placed, out_specs=P("seq", "head"), check_vma=False
    )
```

```python
import math

import jax
import jax.numpy as jnp
from jax import lax
from jax.experimental import pallas as pl
from jax.experimental.pallas import tpu as pltpu
from jax.sharding import PartitionSpec as P

HDIM = 128
TEAM = 2
VMEM = pltpu.VMEM
F32 = jnp.float32
BF16 = jnp.bfloat16


def kernel_call(body, outs, args, scratch=(), flops=0, spaces=None, out_spaces=None):
    spaces = spaces or [VMEM] * len(args)
    out_spaces = out_spaces or [VMEM] * len(outs)
    moved = sum(math.prod(a.shape) * a.dtype.itemsize for a in list(args) + list(outs))
    return pl.pallas_call(
        body,
        out_shape=outs,
        in_specs=[pl.BlockSpec(memory_space=space) for space in spaces],
        out_specs=[pl.BlockSpec(memory_space=space) for space in out_spaces],
        scratch_shapes=list(scratch),
        compiler_params=pltpu.CompilerParams(vmem_limit_bytes=40 * 1024 * 1024),
        cost_estimate=pl.CostEstimate(flops=flops, bytes_accessed=moved, transcendentals=0),
    )(*args)


def place():
    return lax.rem(lax.axis_index("seq"), TEAM)


def cut_keys_values(k_in, v_in, lengths):
    tokens, channels = k_in.shape
    share = channels // TEAM
    row = lengths.reshape(1, lengths.shape[0])

    def body(k_ref, v_ref, row_hbm, own_ref, k_other_ref, v_other_ref, starts_ref, row_ref, sems):
        me = place()
        own = pl.ds(pl.multiple_of(me * share, share), share)
        other = pl.ds(pl.multiple_of((1 - me) * share, share), share)
        moves = [
            (k_ref.at[:, other], k_other_ref),
            (v_ref.at[:, other], v_other_ref),
            (row_hbm, row_ref),
            (k_ref.at[:, own], own_ref.at[0]),
            (v_ref.at[:, own], own_ref.at[1]),
        ]
        copies = [
            pltpu.make_async_copy(source, target, sems.at[i])
            for i, (source, target) in enumerate(moves)
        ]
        for copy in copies:
            copy.start()
        copies[2].wait()
        base = (lax.axis_index("seq") - me) * tokens
        starts_ref[...] = document_starts(row_ref[...], base, tokens)
        for i in (0, 1, 3, 4):
            copies[i].wait()

    sds = jax.ShapeDtypeStruct
    outs = [
        sds((2, tokens, share), BF16),
        sds((tokens, share), BF16),
        sds((tokens, share), BF16),
        sds((TEAM, tokens), jnp.int32),
    ]
    scratch = [VMEM(row.shape, jnp.int32), pltpu.SemaphoreType.DMA((5,))]
    args = [pltpu.with_memory_space_constraint(a, pltpu.HBM) for a in (k_in, v_in, row)]
    return kernel_call(body, outs, args, scratch, spaces=[pl.ANY] * 3)


def cut_queries(q_in):
    tokens, channels = q_in.shape
    share = channels // TEAM

    def body(ref, own_ref, other_ref):
        me = place()
        own_ref[...] = ref[:, pl.ds(pl.multiple_of(me * share, share), share)].T
        other_ref[...] = ref[:, pl.ds(pl.multiple_of((1 - me) * share, share), share)].T

    return kernel_call(body, [jax.ShapeDtypeStruct((share, tokens), BF16)] * 2, [q_in])


def bands(row):
    taps = row.shape[1]
    turned = pltpu.roll(jnp.broadcast_to(row, (taps, taps)), 0, 1, stride=1, stride_axis=0)
    lag = lax.broadcasted_iota(jnp.int32, (taps, taps), 1) - lax.broadcasted_iota(
        jnp.int32, (taps, taps), 0
    )
    zero = jnp.zeros_like(turned)
    earlier = jnp.where(lag < 0, turned, zero).astype(BF16)
    current = jnp.where(lag >= 0, turned, zero).astype(BF16)
    return jnp.concatenate([earlier, current], 0)


def filter_rows(filter_ref, part, me):
    team_groups = filter_ref.shape[1] // TEAM
    first = pl.multiple_of(me * team_groups, team_groups)
    return filter_ref[part, pl.ds(first, team_groups), :].astype(F32)


def attend_heads(q_cols, k_rows, v_cols, starts):
    span, tokens = k_rows[0].shape[0], q_cols[0].shape[1]
    key_pos = lax.broadcasted_iota(jnp.int32, (span, tokens), 0) - tokens
    query_pos = lax.broadcasted_iota(jnp.int32, (span, tokens), 1)
    allowed = (key_pos >= starts) & (key_pos <= query_pos)
    scores = [jnp.dot(k, q, preferred_element_type=F32) for k, q in zip(k_rows, q_cols)]
    scores = [jnp.where(allowed, s * (1.0 / math.sqrt(HDIM)), -1e30) for s in scores]
    weights = [jnp.exp(s - jnp.max(s, axis=0, keepdims=True)) for s in scores]
    totals = [jnp.sum(w, axis=0, keepdims=True) for w in weights]
    mixed = [
        jnp.dot(v, w.astype(BF16), preferred_element_type=F32) for v, w in zip(v_cols, weights)
    ]
    return [(m / t).astype(BF16) for m, t in zip(mixed, totals)]


def document_starts(lengths, base, tokens):
    docs = lengths.shape[1]
    until = lax.broadcasted_iota(jnp.int32, (docs, docs), 1) <= lax.broadcasted_iota(
        jnp.int32, (docs, docs), 0
    )
    spread = jnp.broadcast_to(lengths.astype(F32), (docs, docs))
    ends = jnp.sum(jnp.where(until, spread, 0.0), axis=1, keepdims=True)
    rows = []
    for block in range(TEAM):
        first = base + block * tokens
        pos = (lax.broadcasted_iota(jnp.int32, (docs, tokens), 1) + first).astype(F32)
        begun = jnp.max(jnp.where(ends <= pos, ends, 0.0), axis=0, keepdims=True)
        rows.append(begun.astype(jnp.int32) - first)
    return jnp.concatenate(rows, 0)


def gated(x_now, conv):
    return (x_now.astype(F32) * conv).astype(BF16)


def second_queries(q_own, q_got, after):
    def body(own_ref, got_ref, after_ref, out_ref):
        me = place()

        @pl.when(me == 0)
        def _():
            out_ref[...] = got_ref[...]

        @pl.when(me != 0)
        def _():
            out_ref[...] = own_ref[...]

    outs = [jax.ShapeDtypeStruct(q_own.shape, BF16)]
    flops = 2 * 3 * q_own.size * 256 * 8
    return kernel_call(body, outs, [q_own, q_got, after], (), flops, [VMEM, VMEM, pl.ANY])[0]


def second_conv(q_own, q_got, kv_own, kv_got, filters):
    share, tokens = q_own.shape
    team_groups = filters.shape[1] // TEAM
    width = share // team_groups

    def body(q_own_ref, q_got_ref, kv_own_ref, kv_got_ref, filter_ref, raw_ref, ear_ref, part_ref, q1_ref, k1_ref, v1_ref, x_ref, y_ref):
        me = place()
        other = 1 - me
        x_ref[me, 0] = q_own_ref[...]
        x_ref[me, 1] = kv_own_ref[0].T
        x_ref[me, 2] = kv_own_ref[1].T
        x_ref[other, 0] = q_got_ref[...]
        x_ref[other, 1] = kv_got_ref[0].T
        x_ref[other, 2] = kv_got_ref[1].T
        raw_ref[...] = x_ref[0]
        for part in range(3):
            rows = filter_rows(filter_ref, part, me)
            for group in range(team_groups):
                at = slice(group * width, (group + 1) * width)
                now = x_ref[1, part, at]
                before = x_ref[0, part, at]
                band = bands(rows[group : group + 1])
                left = jnp.concatenate([before, now], 1)
                if part == 0:
                    alone = jnp.concatenate([jnp.zeros_like(before), before], 1)
                    left = jnp.concatenate([left, alone], 0)
                    ear_ref[group * tokens : (group + 1) * tokens, :] = band[:tokens]
                conv = jnp.dot(left, band, preferred_element_type=F32)
                y_ref[part, at] = gated(now, conv[:width])
                if part == 0:
                    part_ref[at] = conv[width:]
        q1_ref[...] = y_ref[0]
        v1_ref[...] = y_ref[2]
        for first in range(0, share, HDIM):
            k1_ref[:, first : first + HDIM] = y_ref[1, first : first + HDIM].T

    sds = jax.ShapeDtypeStruct
    outs = [
        sds((3, share, tokens), BF16),
        sds((team_groups * tokens, tokens), BF16),
        sds((share, tokens), F32),
        sds((share, tokens), BF16),
        sds((tokens, share), BF16),
        sds((share, tokens), BF16),
    ]
    scratch = [VMEM((TEAM, 3, share, tokens), BF16), VMEM((3, share, tokens), BF16)]
    flops = 2 * 3 * share * tokens * 2 * tokens * 8
    return kernel_call(body, outs, [q_own, q_got, kv_own, kv_got, filters], scratch, flops)


def square_row(head_out):
    wide = head_out.astype(F32)
    return jnp.sum(wide * wide, axis=0, keepdims=True)


def rim_keys(rim_own, rim_got, raw, q1, k1, v1, filters, starts):
    share, tokens = q1.shape
    team_groups = filters.shape[1] // TEAM
    width = share // team_groups

    def body(own_ref, got_ref, raw_ref, q1_ref, k1_ref, v1_ref, filter_ref, starts_ref, k_ref, v_ref, out_ref, sum_ref, rim_ref, y_ref):
        me = place()
        for part in range(2):
            rim_ref[me, part * share : (part + 1) * share] = own_ref[part].T
            rim_ref[1 - me, part * share : (part + 1) * share] = got_ref[part].T
        for part in (1, 2):
            rows = filter_rows(filter_ref, part, me)
            for group in range(team_groups):
                at = slice(group * width, (group + 1) * width)
                base = (part - 1) * share + group * width
                further = rim_ref[0, base : base + width]
                before = rim_ref[1, base : base + width]
                now = raw_ref[part, at]
                left = jnp.concatenate(
                    [jnp.concatenate([further, before], 1), jnp.concatenate([before, now], 1)], 0
                )
                conv = jnp.dot(left, bands(rows[group : group + 1]), preferred_element_type=F32)
                far = gated(before, conv[:width])
                near = gated(now, conv[width:])
                if part == 1:
                    y_ref[at, :tokens] = far
                    y_ref[at, tokens:] = near
                else:
                    v_ref[at, :tokens] = far
                    v_ref[at, tokens:] = near
        heads = [slice(first, first + HDIM) for first in range(0, share, HDIM)]
        k_rows = []
        for at in heads:
            k_ref[:tokens, at] = y_ref[at, :tokens].T
            near = y_ref[at, tokens:].T
            k_ref[tokens:, at] = near
            k_rows.append(jnp.concatenate([near, k1_ref[:, at]], 0))
        outs = attend_heads(
            [q1_ref[at, :] for at in heads],
            k_rows,
            [jnp.concatenate([v_ref[at, tokens:], v1_ref[at, :]], 1) for at in heads],
            starts_ref[1:2, :],
        )
        total = jnp.zeros((1, tokens), F32)
        for at, out in zip(heads, outs):
            out_ref[:, at] = out.T
            total = total + square_row(out)
        sum_ref[...] = jnp.broadcast_to(total, (8, tokens))

    sds = jax.ShapeDtypeStruct
    outs = [
        sds((2 * tokens, share), BF16),
        sds((share, 2 * tokens), BF16),
        sds((tokens, share), BF16),
        sds((8, tokens), F32),
    ]
    scratch = [VMEM((TEAM, 2 * share, tokens), BF16), VMEM((share, 2 * tokens), BF16)]
    args = [rim_own, rim_got, raw, q1, k1, v1, filters, starts]
    return kernel_call(body, outs, args, scratch, 2 * 2 * share * tokens * 2 * tokens * 8)


def first_attention(rim_q, raw, ear, part, keys, values, second, second_sum, starts):
    share, tokens = rim_q.shape
    team_groups = ear.shape[0] // tokens
    width = share // team_groups

    def body(rim_ref, raw_ref, ear_ref, part_ref, k_ref, v_ref, second_ref, second_sum_ref, starts_ref, keep_ref, send_ref, sum_ref, y_ref, out_ref):
        me = place()
        for group in range(team_groups):
            at = slice(group * width, (group + 1) * width)
            band = ear_ref[group * tokens : (group + 1) * tokens, :]
            conv = part_ref[at] + jnp.dot(rim_ref[at], band, preferred_element_type=F32)
            y_ref[at] = gated(raw_ref[0, at], conv)
        heads = [slice(first, first + HDIM) for first in range(0, share, HDIM)]
        outs = attend_heads(
            [y_ref[at] for at in heads],
            [k_ref[:, at] for at in heads],
            [v_ref[at, :] for at in heads],
            starts_ref[0:1, :],
        )
        total = jnp.zeros((1, tokens), F32)
        for at, out in zip(heads, outs):
            out_ref[0, :, at] = out.T
            total = total + square_row(out)
        out_ref[1] = second_ref[...]
        row = lax.broadcasted_iota(jnp.int32, (8, tokens), 0)
        sum_ref[...] = jnp.where(row == 0, jnp.broadcast_to(total, (8, tokens)), second_sum_ref[...])
        keep_ref[...] = out_ref[me]
        send_ref[...] = out_ref[1 - me]

    outs = [jax.ShapeDtypeStruct((tokens, share), BF16)] * 2
    outs += [jax.ShapeDtypeStruct((8, tokens), F32)]
    scratch = [VMEM((share, tokens), BF16), VMEM((TEAM, tokens, share), BF16)]
    args = [rim_q, raw, ear, part, keys, values, second, second_sum, starts]
    return kernel_call(body, outs, args, scratch, 2 * share * tokens * 2 * tokens * 8)


def scaled(parts, sums, gain, total_channels, count_got):
    tokens, share = parts[0].shape
    count = len(sums)

    pieces = 4
    rows = tokens // pieces

    def body(*refs):
        part_refs, sum_refs = refs[:TEAM], refs[TEAM : TEAM + count]
        gain_ref, out_ref, held, sems = refs[TEAM + count :]
        me = place()
        total = jnp.zeros((1, tokens), F32)
        for ref in sum_refs:
            total = total + ref[pl.ds(me, 1), :]
        total = jnp.broadcast_to(total, (128, tokens)).T
        gains = [
            gain_ref[:, pl.ds(pl.multiple_of(lax.bitwise_xor(me, step) * share, share), share)]
            for step in range(TEAM)
        ]
        copies = []
        for piece in range(pieces):
            at = slice(piece * rows, (piece + 1) * rows)
            wides = [ref[at].astype(F32) for ref in part_refs]
            sums = total[at]
            if count_got:
                sums = sums + jnp.sum(wides[1] * wides[1], axis=1, keepdims=True)
            scale = lax.rsqrt(sums / total_channels + 1e-06)
            scale = jnp.concatenate([scale] * (share // 128), 1)
            for step in range(TEAM):
                first = pl.multiple_of(lax.bitwise_xor(me, step) * share, share)
                done = (wides[step] * scale * gains[step].astype(F32)).astype(BF16)
                held[at, pl.ds(first, share)] = done
            copy = pltpu.make_async_copy(held.at[at], out_ref.at[at], sems.at[piece])
            copy.start()
            copies.append(copy)
        for copy in copies:
            copy.wait()

    out = jax.ShapeDtypeStruct((tokens, TEAM * share), BF16)
    args = list(parts) + list(sums) + [gain.reshape(1, TEAM * share)]
    scratch = [VMEM((tokens, TEAM * share), BF16), pltpu.SemaphoreType.DMA((pieces,))]
    return kernel_call(body, [out], args, scratch, out_spaces=[pltpu.HBM])[0]


def swapped(value):
    count = lax.axis_size("seq")
    return lax.ppermute(value, "seq", [(i, i ^ 1) for i in range(count)])


def onward(value):
    count = lax.axis_size("seq")
    return lax.ppermute(value, "seq", [(i, i + TEAM) for i in range(count - TEAM)])


def per_device(q_in, k_in, v_in, filters, lengths, gain):
    tokens, channels = q_in.shape
    kv_own, k_other, v_other, starts = cut_keys_values(k_in, v_in, lengths)
    k_got = swapped(k_other)
    v_got = swapped(v_other)
    q_own, q_other = cut_queries(q_in)
    q_other, k_got = lax.optimization_barrier((q_other, k_got))
    q_got = swapped(q_other)
    rim_own = onward(kv_own)
    kv_got = jnp.stack([k_got, v_got])
    rim_got = onward(kv_got)
    rim_q = onward(second_queries(q_own, q_got, kv_got))
    raw, ear, part, q1, k1, v1 = second_conv(q_own, q_got, kv_own, kv_got, filters)
    keys, values, second, second_sum = rim_keys(rim_own, rim_got, raw, q1, k1, v1, filters, starts)
    keep, send, own = first_attention(
        rim_q, raw, ear, part, keys, values, second, second_sum, starts
    )
    mine = [keep, swapped(send)]
    head_count = lax.axis_size("head")
    if head_count == 2:
        cross = [(i, i ^ 3) for i in range(2 * lax.axis_size("seq"))]
        sums = [
            own,
            lax.ppermute(own, "head", [(0, 1), (1, 0)]),
            lax.ppermute(own, ("seq", "head"), cross),
        ]
        return scaled(mine, sums, gain, channels * head_count, True)
    own = lax.psum(own, "head")
    return scaled(mine, [own, swapped(own)], gain, channels * head_count, False)


def solution(mesh):
    placed = (
        P("seq", "head"),
        P("seq", "head"),
        P("seq", "head"),
        P(None, "head", None),
        P(),
        P("head"),
    )
    return jax.shard_map(
        per_device, mesh=mesh, in_specs=placed, out_specs=P("seq", "head"), check_vma=False
    )
```
